32 devices in a mesh: gx: 16 (over z, y, core), gy: 2 (over x).
Axes of the slice: x: 2, y: 2, z: 4, core: 2. Of those that a mesh axis runs over, the one named last changes fastest.
Arguments:
- kernel: bfloat16 [32768, 512], P(('gx', 'gy')), may hold values from -0.25 to 0.25
- margin: bfloat16 [32768, 512], P(('gx', 'gy')), may hold values from -0.25 to 0.25
- hamiltonian: bfloat16 [32768, 512], P(('gx', 'gy')), may hold values from -9 to 9
- columns: int32 [512, 8], replicated, may hold values from -1 to 511, as said below
Outputs:
- gradient_term: float32 [32768, 512], P(('gx', 'gy'))
The draws below stay inside these ranges and needn't reach their ends.
Inputs may be any that keep to these rules, and one draw needn't show every extreme that they name: `columns`: clusters are numbered device by device, 16 each, device number = gx index * (devices along gy) + gy index. Slot 0 of row i names i itself; the live ids of a row are distinct, live slots come first and the rest hold -1; every device has a row with all 8 slots live. A row of the device at (x, y) names only clusters of its own device and clusters number r + 4 * (2 p + q) (r < 4, counted within the device) of the device at (x + s, y + t), indices wrapping around, with s and t in -1, 0, 1, where p = 1 if s = -1, p = 0 if s = 1, either if s = 0, and likewise q from t.
All inputs are finite; a program needn't handle non-finite values.
Results may differ from the reference program's by a relative error of at most 0.005.
Values may be sent and summed in bfloat16 or wider, within the bound.
A program may use at most 128 MiB of HBM per device.

```python
import math
import jax
import jax.numpy as jnp
import numpy as np
from jax import lax

BS = 64
NB = 8
EDGE = 4
BLK_DEV = 16
NBLK = 512
N_GX = 16
N_GY = 2


def draw_columns(key, part):
    device_count = N_GX * N_GY
    device_ids = jnp.arange(device_count, dtype=jnp.int32)
    along_x = device_ids // N_GY
    along_y = device_ids % N_GY
    offsets = jnp.array(np.array([-1, 0, 0, 1], np.int32))
    corner_side = jnp.array(np.array([1, 0, 1, 0], np.int32))
    source_x = (along_x[:, None] + offsets[None, :]) % N_GX
    source_y = (along_y[:, None] + offsets[None, :]) % N_GY
    owners = source_x[:, :, None] * N_GY + source_y[:, None, :]
    quadrant = (2 * corner_side[:, None] + corner_side[None, :]) * EDGE
    ghosts = owners[:, :, :, None] * BLK_DEV + quadrant[None, :, :, None] + jnp.arange(EDGE, dtype=jnp.int32)[None, None, None, :]
    ghosts = ghosts.reshape(device_count, 16 * EDGE)
    locals_ids = device_ids[:, None] * BLK_DEV + jnp.arange(BLK_DEV, dtype=jnp.int32)[None, :]
    candidates = jnp.concatenate([locals_ids, ghosts], axis=1)
    width = BLK_DEV + 16 * EDGE
    earlier = jnp.arange(width)[:, None] > jnp.arange(width)[None, :]
    repeated = jnp.any((candidates[:, :, None] == candidates[:, None, :]) & earlier[None, :, :], axis=2)
    key_score = jax.random.fold_in(key, 11)
    key_count = jax.random.fold_in(key, 23)
    scores = jax.random.randint(key_score, (device_count, BLK_DEV, width), 0, 1 << 20) * width + jnp.arange(width, dtype=jnp.int32)[None, None, :]
    self_slot = jnp.arange(width)[None, :] == jnp.arange(BLK_DEV)[:, None]
    scores = jnp.where(self_slot[None, :, :], 1 << 30, scores)
    scores = jnp.where(repeated[:, None, :], -1, scores)
    scores_top, chosen = lax.top_k(scores, NB)
    spread = jnp.broadcast_to(candidates[:, None, :], (device_count, BLK_DEV, width))
    picked = jnp.take_along_axis(spread, chosen, axis=2)
    lowest = NB // 2 + NB // 2 * along_x // N_GX
    counts = jax.random.randint(key_count, (device_count, BLK_DEV), lowest[:, None], NB + 1)
    counts = jnp.where(jnp.arange(BLK_DEV)[None, :] == BLK_DEV - 1, NB, counts)
    picked = jnp.where(jnp.arange(NB)[None, None, :] < counts[:, :, None], picked, -1)
    return picked.reshape(device_count * BLK_DEV, NB).astype(jnp.int32)


def block_scale(own_key, shape, shards, smallest, largest):
    factor_of, own = 1.0, jax.random.fold_in(own_key, 6)
    for dim, blocks in shards:
        steps = jnp.exp(jax.random.uniform(jax.random.fold_in(own, dim), (blocks,), jnp.float32, smallest / len(shards), largest / len(shards)))
        factor_of = factor_of * jnp.repeat(steps, shape[dim] // blocks).reshape([-1 if axis == dim else 1 for axis in range(len(shape))])
    return factor_of


def bell_draw(own_key, extent, deviation, most, split=(), held_as=jnp.bfloat16):
    values = deviation * jax.random.normal(own_key, extent, jnp.float32)
    if split:
        values = values * block_scale(own_key, extent, split, -0.22, 0.18)
    return jnp.clip(values, -most, most).astype(held_as)


def setup_inputs(seed: int = 0) -> dict:
    splits = jax.random.split(jax.random.key(seed), 5)
    kernel = bell_draw(splits[0], (NBLK * BS, NB * BS), (NB * BS) ** -0.5, 0.25, ((0, 32),))
    margin = bell_draw(splits[1], (NBLK * BS, NB * BS), (NB * BS) ** -0.5, 0.25, ((0, 32),))
    hamiltonian = bell_draw(splits[2], (NBLK * BS, NB * BS), 1.5, 9.0, ((0, 32),))
    columns = draw_columns(jax.random.fold_in(splits[4], 71), 0)
    return {"kernel": kernel, "margin": margin, "hamiltonian": hamiltonian, "columns": columns}


def pattern_product(left, right, columns):
    total = columns.shape[0]
    blocks = right.reshape(total, BS, NB, BS)
    group = math.gcd(8, total)
    slot_ids = jnp.arange(NB, dtype=jnp.int32)

    def product_row(left_row, slot_row):
        is_live = slot_row >= 0
        where_row = jnp.where(is_live, slot_row, 0).astype(jnp.int32)
        far_columns = columns[where_row]
        matched = (far_columns[:, :, None] == slot_row[None, None, :]) & is_live[:, None, None] & is_live[None, None, :]
        has_match = jnp.any(matched, axis=1)
        slot_index = jnp.sum(jnp.where(matched, slot_ids[None, :, None], 0), axis=1).astype(jnp.int32)
        gathered = blocks[where_row[:, None], :, slot_index, :]
        gathered = jnp.where(has_match[:, :, None, None], gathered.astype(jnp.float32), jnp.float32(0.0))
        return jnp.einsum("ras,abst->rbt", left_row.astype(jnp.float32), gathered)

    def group_rows(pieces):
        return jax.vmap(product_row)(pieces[0], pieces[1])

    left_groups = left.reshape(total // group, group, BS, NB, BS)
    slot_groups = columns.reshape(total // group, group, NB)
    result = lax.map(group_rows, (left_groups, slot_groups))
    return result.reshape(total * BS, NB * BS)


def reference(kernel, margin, hamiltonian, columns):
    lead_product = pattern_product(kernel, margin, columns).astype(jnp.bfloat16)
    cubic = pattern_product(lead_product, kernel, columns).astype(jnp.bfloat16)
    fifth = pattern_product(lead_product, cubic, columns)
    purified = (3.0 * cubic.astype(jnp.float32) - 2.0 * fifth).astype(jnp.bfloat16)
    return pattern_product(hamiltonian, purified, columns)
```

```python
import functools

import jax
import jax.numpy as jnp
import numpy as np
from jax import lax
from jax.experimental import pallas as pl
from jax.experimental.pallas import tpu as pltpu
from jax.sharding import PartitionSpec as P

BS = 64
NB = 8
EDGE = 4
BLK_DEV = 16
OWN = BLK_DEV * NB
DIRS = ((0, -1), (0, 1), (-1, 0), (1, 0), (-1, -1), (-1, 1), (1, -1), (1, 1))
CORNERS = {-1: (1,), 0: (0, 1), 1: (0,)}


def direction_rows(s, t):
    return [EDGE * (2 * p + q) + r for p in CORNERS[s] for q in CORNERS[t] for r in range(EDGE)]


ROWS = [direction_rows(s, t) for s, t in DIRS]
FULL = tuple(len(rows) * NB for rows in ROWS)
SMALL = (32, 32, 24, 24, 16, 16, 16, 16)
GHOST = sum(FULL)
STARTS = np.cumsum((0,) + FULL)
WIDEST = max(FULL)


def starts_of(caps):
    return [int(v) for v in np.cumsum((0,) + caps)]


def tables(columns, along_gx, along_gy, gx_index, gy_index):
    count = along_gx * along_gy
    ids = jnp.arange(count * BLK_DEV, dtype=jnp.int32).reshape(along_gx, along_gy, BLK_DEV)
    slots = columns.reshape(along_gx, along_gy, BLK_DEV, NB)
    ghost_ids, ghost_slots = [], []
    for (s, t), rows in zip(DIRS, ROWS):
        for source, kept in ((ids[..., None], ghost_ids), (slots, ghost_slots)):
            moved = jnp.roll(source, (-s, -t), (0, 1))
            pieces = [moved[:, :, r : r + EDGE] for r in rows[::EDGE]]
            kept.append(jnp.concatenate(pieces, axis=2))
    ghost_slots = jnp.concatenate(ghost_slots, axis=2).reshape(count, GHOST)
    ghost_ids = jnp.concatenate(ghost_ids, axis=2)
    ghost_ids = jnp.broadcast_to(ghost_ids, ghost_ids.shape[:3] + (NB,)).reshape(count, GHOST)
    live = jnp.where(slots >= 0, slots, -2).reshape(count, BLK_DEV, NB)
    names_row = jnp.zeros((count, BLK_DEV, GHOST), bool)
    names_column = jnp.zeros((count, BLK_DEV, GHOST), bool)
    for b in range(NB):
        names_row |= live[:, :, b, None] == ghost_ids[:, None, :]
        names_column |= live[:, :, b, None] == ghost_slots[:, None, :]
    need = jnp.any(names_row & names_column, axis=1)
    segment = np.repeat(np.arange(len(DIRS)), FULL)
    before = (segment[:, None] == segment[None, :]) & (np.arange(GHOST)[:, None] < np.arange(GHOST)[None, :])
    ones = need.astype(jnp.bfloat16)
    rank = jnp.dot(ones, jnp.asarray(before, jnp.bfloat16), preferred_element_type=jnp.float32).astype(jnp.int32)
    limit = jnp.asarray(np.repeat(SMALL, FULL).astype(np.int32))
    fits = jnp.all(jnp.where(need, rank < limit, True))
    ranked = jnp.where(need, rank, -1)

    own_rank = lax.dynamic_index_in_dim(ranked, gx_index * along_gy + gy_index, 0, keepdims=False)
    by_device = ranked.reshape(along_gx, along_gy, GHOST)
    sent_rank = jnp.concatenate(
        [jnp.roll(by_device[:, :, lo:hi], (s, t), (0, 1)) for (s, t), lo, hi in zip(DIRS, STARTS[:-1], STARTS[1:])],
        axis=2,
    ).reshape(count, GHOST)
    sent_rank = lax.dynamic_index_in_dim(sent_rank, gx_index * along_gy + gy_index, 0, keepdims=False)
    block = np.concatenate([[1 + r * NB + c for r in rows for c in range(NB)] for rows in ROWS])
    chosen = (sent_rank[:, None] == jnp.arange(WIDEST, dtype=jnp.int32)[None, :]).astype(jnp.bfloat16)
    weights = (segment[None, :] == np.arange(len(DIRS))[:, None]) * block[None, :]
    sends = jnp.dot(jnp.asarray(weights, jnp.bfloat16), chosen, preferred_element_type=jnp.float32)
    sends = sends.astype(jnp.int32)

    me = gx_index * along_gy + gy_index
    own_slots = lax.dynamic_index_in_dim(columns.reshape(count, BLK_DEV, NB), me, 0, keepdims=False)
    my_ghost_slots = lax.dynamic_index_in_dim(ghost_slots, me, 0, keepdims=False)
    my_ghost_ids = lax.dynamic_index_in_dim(ghost_ids, me, 0, keepdims=False)
    flat_slots = jnp.concatenate([own_slots.reshape(-1), my_ghost_slots])
    row_ids = jnp.concatenate([jnp.repeat(me * BLK_DEV + jnp.arange(BLK_DEV, dtype=jnp.int32), NB), my_ghost_ids])
    wanted = jnp.where(own_slots >= 0, own_slots, -2)
    of_row = wanted[:, :, None] == row_ids[None, None, :]
    of_column = wanted[:, :, None] == flat_slots[None, None, :]

    def places(caps):
        offset = np.repeat(starts_of(caps)[:-1], FULL) + 1 + OWN
        ghost = jnp.where(own_rank >= 0, own_rank + jnp.asarray(offset, jnp.int32), 0)
        place = jnp.concatenate([1 + jnp.arange(OWN, dtype=jnp.int32), ghost])
        both = of_row[:, :, None, :] & of_column[:, None, :, :]
        return jnp.sum(jnp.where(both, place[None, None, None, :], 0), axis=3).reshape(-1)

    def send_list(caps):
        return jnp.concatenate([sends[d, :cap] for d, cap in enumerate(caps)])

    return fits, places, send_list


def purify(sizes, caps, place_ref, send_ref, kernel_ref, margin_ref, ham_ref, out_ref,
           blocks, other, lead, cubic, out_box, in_box, send_sem, recv_sem):
    along_gx, along_gy = sizes
    pair_starts = [v // 2 for v in starts_of(caps)]
    pairs = pair_starts[-1]
    gx_index, gy_index = lax.axis_index("gx"), lax.axis_index("gy")
    targets = [
        (lax.rem(gx_index - s + along_gx, along_gx), lax.rem(gy_index - t + along_gy, along_gy)) for s, t in DIRS
    ]
    low = lax.broadcasted_iota(jnp.int32, (BS, 2 * BS), 1) < BS

    def own(source, into):
        @pl.loop(0, BLK_DEV)
        def _(i):
            rows = pl.ds(pl.multiple_of(i * BS, BS), BS)
            for c in range(NB):
                block = source[rows, c * BS : (c + 1) * BS]
                into[1 + i * NB + c] = jnp.concatenate([block, block], axis=1)

    def exchange(turn, source):
        slot = turn % 2

        @pl.loop(0, pairs // 2)
        def _(h):
            for j in range(2):
                first = source[send_ref[4 * h + 2 * j]]
                second = source[send_ref[4 * h + 2 * j + 1]]
                out_box[slot, 2 * h + j] = jnp.where(low, first, second)

        copies = []
        for d, target in enumerate(targets):
            part = pl.ds(pair_starts[d], pair_starts[d + 1] - pair_starts[d])
            copies.append(
                pltpu.make_async_remote_copy(
                    src_ref=out_box.at[slot, part],
                    dst_ref=in_box.at[turn, part],
                    send_sem=send_sem.at[turn, d],
                    recv_sem=recv_sem.at[turn, d],
                    device_id=target,
                    device_id_type=pl.DeviceIdType.MESH,
                )
            )
        return copies

    def arrive(turn, copies, into):
        for copy in copies:
            copy.wait_recv()

        @pl.loop(0, pairs // 2)
        def _(h):
            for j in range(2):
                pair = in_box[turn, 2 * h + j]
                first, second = pair[:, :BS], pair[:, BS:]
                at = 1 + OWN + 4 * h + 2 * j
                into[at] = jnp.concatenate([first, first], axis=1)
                into[at + 1] = jnp.concatenate([second, second], axis=1)

    def product(left, right, finish):
        @pl.loop(0, BLK_DEV)
        def _(i):
            rows = pl.ds(pl.multiple_of(i * BS, BS), BS)
            left_rows = left[rows, :]
            for half in range(2):
                wide = []
                for b in (4 * half, 4 * half + 2):
                    tall = []
                    for a in range(NB):
                        at = (i * NB + a) * NB + b
                        tall.append(jnp.where(low, right[place_ref[at]], right[place_ref[at + 1]]))
                    wide.append(jnp.concatenate(tall, axis=0))
                result = jnp.dot(left_rows, jnp.concatenate(wide, axis=1), preferred_element_type=jnp.float32)
                finish(rows, slice(4 * half * BS, 4 * (half + 1) * BS), result)

    def put_lead(rows, cols, result):
        lead[rows, cols] = result.astype(jnp.bfloat16)

    def put_cubic(rows, cols, result):
        cubic[rows, cols] = result.astype(jnp.bfloat16)

    def put_purified(rows, cols, result):
        value = 3.0 * cubic[rows, cols].astype(jnp.float32) - 2.0 * result
        cubic[rows, cols] = value.astype(jnp.bfloat16)

    def put_out(rows, cols, result):
        out_ref[rows, cols] = result

    barrier = pltpu.get_barrier_semaphore()
    for target, (s, t) in zip(targets, DIRS):
        pl.semaphore_signal(barrier, inc=1, device_id=target, device_id_type=pl.DeviceIdType.MESH)
    zero = jnp.zeros((BS, 2 * BS), jnp.bfloat16)
    blocks[0] = zero
    other[0] = zero
    own(margin_ref, blocks)
    first = exchange(0, blocks)
    pl.semaphore_wait(barrier, len(DIRS))
    for copy in first:
        copy.start()
    own(kernel_ref, other)
    second = exchange(1, other)
    for copy in second:
        copy.start()
    arrive(0, first, blocks)
    product(kernel_ref, blocks, put_lead)
    arrive(1, second, other)
    product(lead, other, put_cubic)
    own(cubic, blocks)
    for copy in first:
        copy.wait_send()
    third = exchange(2, blocks)
    for copy in third:
        copy.start()
    arrive(2, third, blocks)
    product(lead, blocks, put_purified)
    own(cubic, other)
    for copy in second:
        copy.wait_send()
    fourth = exchange(3, other)
    for copy in fourth:
        copy.start()
    arrive(3, fourth, other)
    product(ham_ref, other, put_out)
    for copy in third + fourth:
        copy.wait_send()


def call(sizes, caps, collective_id, places, send_list, kernel, margin, hamiltonian):
    pairs = sum(caps) // 2
    rows, width = kernel.shape
    in_vmem = pl.BlockSpec(memory_space=pltpu.VMEM)
    in_smem = pl.BlockSpec(memory_space=pltpu.SMEM)
    block_count = 1 + OWN + sum(caps)
    return pl.pallas_call(
        functools.partial(purify, sizes, caps),
        out_shape=jax.ShapeDtypeStruct((rows, width), jnp.float32),
        in_specs=[in_smem, in_smem, in_vmem, in_vmem, in_vmem],
        out_specs=in_vmem,
        scratch_shapes=[
            pltpu.VMEM((block_count, BS, 2 * BS), jnp.bfloat16),
            pltpu.VMEM((block_count, BS, 2 * BS), jnp.bfloat16),
            pltpu.VMEM((rows, width), jnp.bfloat16),
            pltpu.VMEM((rows, width), jnp.bfloat16),
            pltpu.VMEM((2, pairs, BS, 2 * BS), jnp.bfloat16),
            pltpu.VMEM((4, pairs, BS, 2 * BS), jnp.bfloat16),
            pltpu.SemaphoreType.DMA((4, len(DIRS))),
            pltpu.SemaphoreType.DMA((4, len(DIRS))),
        ],
        compiler_params=pltpu.CompilerParams(
            collective_id=collective_id, has_side_effects=True, vmem_limit_bytes=56 * 2**20
        ),
    )(places, send_list, kernel, margin, hamiltonian)


def body(sizes, kernel, margin, hamiltonian, columns):
    fits, places, send_list = tables(columns, *sizes, lax.axis_index("gx"), lax.axis_index("gy"))

    def run(caps, collective_id):
        return lambda: call(
            sizes, caps, collective_id, places(caps), send_list(caps), kernel, margin, hamiltonian
        )

    return lax.cond(fits, run(SMALL, 0), run(FULL, 1))


def solution(mesh):
    sizes = (mesh.shape["gx"], mesh.shape["gy"])
    in_specs = (P(("gx", "gy"), None), P(("gx", "gy"), None), P(("gx", "gy"), None), P())
    out_specs = P(("gx", "gy"), None)
    return jax.shard_map(
        functools.partial(body, sizes), mesh=mesh, in_specs=in_specs, out_specs=out_specs, check_vma=False
    )
```

```python
import functools

import jax
import jax.numpy as jnp
import numpy as np
from jax import lax
from jax.experimental import pallas as pl
from jax.experimental.pallas import tpu as pltpu
from jax.sharding import PartitionSpec as P

BS = 64
NB = 8
EDGE = 4
BLK_DEV = 16
OWN = BLK_DEV * NB
DIRS = ((0, -1), (0, 1), (-1, 0), (1, 0), (-1, -1), (-1, 1), (1, -1), (1, 1))
CORNERS = {-1: (1,), 0: (0, 1), 1: (0,)}


def direction_rows(s, t):
    return [EDGE * (2 * p + q) + r for p in CORNERS[s] for q in CORNERS[t] for r in range(EDGE)]


ROWS = [direction_rows(s, t) for s, t in DIRS]
SIZES = [len(rows) * NB for rows in ROWS]
GHOST = sum(SIZES)


def messages(along_gy):
    if along_gy == 2:
        return ((0, 1), (2,), (3,), (4, 5), (6, 7))
    return tuple((d,) for d in range(len(DIRS)))


def full_caps(along_gy):
    return tuple(sum(SIZES[d] for d in group) for group in messages(along_gy))


def small_caps(along_gy):
    return (48, 24, 24, 20, 20) if along_gy == 2 else (32, 32, 24, 24, 16, 16, 16, 16)


def starts_of(caps):
    return [int(v) for v in np.cumsum((0,) + caps)]


def tables(columns, along_gx, along_gy, gx_index, gy_index):
    count = along_gx * along_gy
    groups, full = messages(along_gy), full_caps(along_gy)
    bounds = starts_of(full)
    widest = max(full)
    ids = np.arange(count * BLK_DEV, dtype=np.int32).reshape(along_gx, along_gy, BLK_DEV)
    ids = np.repeat(ids, NB, axis=2)
    lanes = columns.reshape(along_gx, along_gy, OWN)

    def ghosts(lib, source):
        kept = []
        for (s, t), rows in zip(DIRS, ROWS):
            moved = lib.roll(source, (-s, -t), (0, 1))
            kept += [moved[:, :, r * NB : (r + EDGE) * NB] for r in rows[::EDGE]]
        return lib.concatenate(kept, axis=2).reshape(count, GHOST)

    ghost_ids = jnp.asarray(ghosts(np, ids))
    ghost_slots = ghosts(jnp, lanes)
    slots = columns.reshape(count, BLK_DEV, NB)
    live = jnp.where(slots >= 0, slots, -2)
    names_row = jnp.zeros((count, BLK_DEV, GHOST), bool)
    names_column = jnp.zeros((count, BLK_DEV, GHOST), bool)
    for b in range(NB):
        names_row |= live[:, :, b, None] == ghost_ids[:, None, :]
        names_column |= live[:, :, b, None] == ghost_slots[:, None, :]
    need = jnp.any(names_row & names_column, axis=1)
    segment = np.repeat(np.arange(len(groups)), full)
    before = (segment[:, None] == segment[None, :]) & (np.arange(GHOST)[:, None] < np.arange(GHOST)[None, :])
    ones = need.astype(jnp.bfloat16)
    rank = jnp.dot(ones, jnp.asarray(before, jnp.bfloat16), preferred_element_type=jnp.float32).astype(jnp.int32)
    limit = jnp.asarray(np.repeat(small_caps(along_gy), full).astype(np.int32))
    fits = jnp.all(jnp.where(need, rank < limit, True))
    ranked = jnp.where(need, rank, -1)

    own_rank = lax.dynamic_index_in_dim(ranked, gx_index * along_gy + gy_index, 0, keepdims=False)
    by_device = ranked.reshape(along_gx, along_gy, GHOST)
    sent_rank = jnp.concatenate(
        [jnp.roll(by_device[:, :, lo:hi], (s, t), (0, 1)) for (s, t), lo, hi in zip([DIRS[g[0]] for g in groups], bounds[:-1], bounds[1:])],
        axis=2,
    ).reshape(count, GHOST)
    sent_rank = lax.dynamic_index_in_dim(sent_rank, gx_index * along_gy + gy_index, 0, keepdims=False)
    block = np.concatenate([[1 + r * NB + c for r in rows for c in range(NB)] for rows in ROWS])
    chosen = (sent_rank[:, None] == jnp.arange(widest, dtype=jnp.int32)[None, :]).astype(jnp.bfloat16)
    weights = (segment[None, :] == np.arange(len(groups))[:, None]) * block[None, :]
    sends = jnp.dot(jnp.asarray(weights, jnp.bfloat16), chosen, preferred_element_type=jnp.float32)
    sends = sends.astype(jnp.int32)

    me = gx_index * along_gy + gy_index
    own_slots = lax.dynamic_index_in_dim(slots, me, 0, keepdims=False)
    my_ghost_slots = lax.dynamic_index_in_dim(ghost_slots, me, 0, keepdims=False)
    my_ghost_ids = lax.dynamic_index_in_dim(ghost_ids, me, 0, keepdims=False)
    flat_slots = jnp.concatenate([own_slots.reshape(-1), my_ghost_slots])
    row_ids = jnp.concatenate([jnp.repeat(me * BLK_DEV + jnp.arange(BLK_DEV, dtype=jnp.int32), NB), my_ghost_ids])
    wanted = jnp.where(own_slots >= 0, own_slots, -2)
    of_row = wanted[:, :, None] == row_ids[None, None, :]
    of_column = wanted[:, :, None] == flat_slots[None, None, :]

    def places(caps):
        offset = np.repeat(starts_of(caps)[:-1], full) + 1 + OWN
        ghost = jnp.where(own_rank >= 0, own_rank + jnp.asarray(offset, jnp.int32), 0)
        place = jnp.concatenate([1 + jnp.arange(OWN, dtype=jnp.int32), ghost])
        both = of_row[:, :, None, :] & of_column[:, None, :, :]
        return jnp.sum(jnp.where(both, place[None, None, None, :], 0), axis=3).reshape(-1)

    def send_list(caps):
        return jnp.concatenate([sends[d, :cap] for d, cap in enumerate(caps)])

    return fits, places, send_list


def purify(sizes, caps, place_ref, send_ref, kernel_ref, margin_ref, ham_ref, out_ref,
           blocks, other, lead, cubic, out_box, in_box, send_sem, recv_sem):
    along_gx, along_gy = sizes
    pair_starts = [v // 2 for v in starts_of(caps)]
    pairs = pair_starts[-1]
    gx_index, gy_index = lax.axis_index("gx"), lax.axis_index("gy")
    served = [DIRS[group[0]] for group in messages(along_gy)]
    targets = [
        (lax.rem(gx_index - s + along_gx, along_gx), lax.rem(gy_index - t + along_gy, along_gy)) for s, t in served
    ]
    low = lax.broadcasted_iota(jnp.int32, (BS, 2 * BS), 1) < BS

    def own(source, into):
        @pl.loop(0, BLK_DEV)
        def _(i):
            rows = pl.ds(pl.multiple_of(i * BS, BS), BS)
            for c in range(NB):
                block = source[rows, c * BS : (c + 1) * BS]
                into[1 + i * NB + c] = jnp.concatenate([block, block], axis=1)

    def exchange(turn, source):
        slot = turn % 2

        @pl.loop(0, pairs // 2)
        def _(h):
            for j in range(2):
                first = source[send_ref[4 * h + 2 * j]]
                second = source[send_ref[4 * h + 2 * j + 1]]
                out_box[slot, 2 * h + j] = jnp.where(low, first, second)

        copies = []
        for d, target in enumerate(targets):
            part = pl.ds(pair_starts[d], pair_starts[d + 1] - pair_starts[d])
            copies.append(
                pltpu.make_async_remote_copy(
                    src_ref=out_box.at[slot, part],
                    dst_ref=in_box.at[turn, part],
                    send_sem=send_sem.at[turn, d],
                    recv_sem=recv_sem.at[turn, d],
                    device_id=target,
                    device_id_type=pl.DeviceIdType.MESH,
                )
            )
        return copies

    def arrive(turn, copies, into):
        for copy in copies:
            copy.wait_recv()

        @pl.loop(0, pairs // 2)
        def _(h):
            for j in range(2):
                pair = in_box[turn, 2 * h + j]
                first, second = pair[:, :BS], pair[:, BS:]
                at = 1 + OWN + 4 * h + 2 * j
                into[at] = jnp.concatenate([first, first], axis=1)
                into[at + 1] = jnp.concatenate([second, second], axis=1)

    def product(left, right, finish):
        @pl.loop(0, BLK_DEV)
        def _(i):
            rows = pl.ds(pl.multiple_of(i * BS, BS), BS)
            left_rows = left[rows, :]
            for half in range(2):
                wide = []
                for b in (4 * half, 4 * half + 2):
                    tall = []
                    for a in range(NB):
                        at = (i * NB + a) * NB + b
                        tall.append(jnp.where(low, right[place_ref[at]], right[place_ref[at + 1]]))
                    wide.append(jnp.concatenate(tall, axis=0))
                result = jnp.dot(left_rows, jnp.concatenate(wide, axis=1), preferred_element_type=jnp.float32)
                finish(rows, slice(4 * half * BS, 4 * (half + 1) * BS), result)

    def put_lead(rows, cols, result):
        lead[rows, cols] = result.astype(jnp.bfloat16)

    def put_cubic(rows, cols, result):
        cubic[rows, cols] = result.astype(jnp.bfloat16)

    def put_purified(rows, cols, result):
        value = 3.0 * cubic[rows, cols].astype(jnp.float32) - 2.0 * result
        cubic[rows, cols] = value.astype(jnp.bfloat16)

    def put_out(rows, cols, result):
        out_ref[rows, cols] = result

    barrier = pltpu.get_barrier_semaphore()
    for target in targets:
        pl.semaphore_signal(barrier, inc=1, device_id=target, device_id_type=pl.DeviceIdType.MESH)
    zero = jnp.zeros((BS, 2 * BS), jnp.bfloat16)
    blocks[0] = zero
    other[0] = zero
    own(margin_ref, blocks)
    first = exchange(0, blocks)
    pl.semaphore_wait(barrier, len(targets))
    for copy in first:
        copy.start()
    own(kernel_ref, other)
    second = exchange(1, other)
    for copy in second:
        copy.start()
    arrive(0, first, blocks)
    product(kernel_ref, blocks, put_lead)
    arrive(1, second, other)
    product(lead, other, put_cubic)
    own(cubic, blocks)
    for copy in first:
        copy.wait_send()
    third = exchange(2, blocks)
    for copy in third:
        copy.start()
    arrive(2, third, blocks)
    product(lead, blocks, put_purified)
    own(cubic, other)
    for copy in second:
        copy.wait_send()
    fourth = exchange(3, other)
    for copy in fourth:
        copy.start()
    arrive(3, fourth, other)
    product(ham_ref, other, put_out)
    for copy in third + fourth:
        copy.wait_send()


def call(sizes, caps, collective_id, places, send_list, kernel, margin, hamiltonian):
    pairs = sum(caps) // 2
    rows, width = kernel.shape
    in_vmem = pl.BlockSpec(memory_space=pltpu.VMEM)
    in_smem = pl.BlockSpec(memory_space=pltpu.SMEM)
    block_count = 1 + OWN + sum(caps)
    return pl.pallas_call(
        functools.partial(purify, sizes, caps),
        out_shape=jax.ShapeDtypeStruct((rows, width), jnp.float32),
        in_specs=[in_smem, in_smem, in_vmem, in_vmem, in_vmem],
        out_specs=in_vmem,
        scratch_shapes=[
            pltpu.VMEM((block_count, BS, 2 * BS), jnp.bfloat16),
            pltpu.VMEM((block_count, BS, 2 * BS), jnp.bfloat16),
            pltpu.VMEM((rows, width), jnp.bfloat16),
            pltpu.VMEM((rows, width), jnp.bfloat16),
            pltpu.VMEM((2, pairs, BS, 2 * BS), jnp.bfloat16),
            pltpu.VMEM((4, pairs, BS, 2 * BS), jnp.bfloat16),
            pltpu.SemaphoreType.DMA((4, len(caps))),
            pltpu.SemaphoreType.DMA((4, len(caps))),
        ],
        compiler_params=pltpu.CompilerParams(
            collective_id=collective_id, has_side_effects=True, vmem_limit_bytes=56 * 2**20
        ),
    )(places, send_list, kernel, margin, hamiltonian)


def body(sizes, kernel, margin, hamiltonian, columns):
    fits, places, send_list = tables(columns, *sizes, lax.axis_index("gx"), lax.axis_index("gy"))

    def run(caps, collective_id):
        return lambda: call(
            sizes, caps, collective_id, places(caps), send_list(caps), kernel, margin, hamiltonian
        )

    return lax.cond(fits, run(small_caps(sizes[1]), 0), run(full_caps(sizes[1]), 1))


def solution(mesh):
    sizes = (mesh.shape["gx"], mesh.shape["gy"])
    in_specs = (P(("gx", "gy"), None), P(("gx", "gy"), None), P(("gx", "gy"), None), P())
    out_specs = P(("gx", "gy"), None)
    return jax.shard_map(
        functools.partial(body, sizes), mesh=mesh, in_specs=in_specs, out_specs=out_specs, check_vma=False
    )
```

```python
import functools

import jax
import jax.numpy as jnp
import numpy as np
from jax import lax
from jax.experimental import pallas as pl
from jax.experimental.pallas import tpu as pltpu
from jax.sharding import PartitionSpec as P

BS = 64
NB = 8
EDGE = 4
BLK_DEV = 16
OWN = BLK_DEV * NB
DIRS = ((0, -1), (0, 1), (-1, 0), (1, 0), (-1, -1), (-1, 1), (1, -1), (1, 1))
CORNERS = {-1: (1,), 0: (0, 1), 1: (0,)}


def direction_rows(s, t):
    return [EDGE * (2 * p + q) + r for p in CORNERS[s] for q in CORNERS[t] for r in range(EDGE)]


ROWS = [direction_rows(s, t) for s, t in DIRS]
SIZES = [len(rows) * NB for rows in ROWS]
GHOST = sum(SIZES)


def messages(along_gy):
    if along_gy == 2:
        return ((0, 1), (2,), (3,), (4, 5), (6, 7))
    return tuple((d,) for d in range(len(DIRS)))


def full_caps(along_gy):
    return tuple(sum(SIZES[d] for d in group) for group in messages(along_gy))


def tiers(along_gy):
    if along_gy == 2:
        return (44, 24, 24, 18, 18), (56, 28, 28, 24, 24), full_caps(along_gy)
    return (28, 28, 20, 20, 14, 14, 14, 14), (40, 40, 32, 32, 20, 20, 20, 20), full_caps(along_gy)


def starts_of(caps):
    return [int(v) for v in np.cumsum((0,) + caps)]


def tables(columns, along_gx, along_gy, gx_index, gy_index):
    count = along_gx * along_gy
    groups, full = messages(along_gy), full_caps(along_gy)
    bounds = starts_of(full)
    widest = max(full)
    ids = np.arange(count * BLK_DEV, dtype=np.int32).reshape(along_gx, along_gy, BLK_DEV)
    ids = np.repeat(ids, NB, axis=2)
    lanes = columns.reshape(along_gx, along_gy, OWN)

    def ghosts(lib, source):
        kept = []
        for (s, t), rows in zip(DIRS, ROWS):
            moved = lib.roll(source, (-s, -t), (0, 1))
            kept += [moved[:, :, r * NB : (r + EDGE) * NB] for r in rows[::EDGE]]
        return lib.concatenate(kept, axis=2).reshape(count, GHOST)

    ghost_ids = jnp.asarray(ghosts(np, ids))
    ghost_slots = ghosts(jnp, lanes)
    slots = columns.reshape(count, BLK_DEV, NB)
    live = jnp.where(slots >= 0, slots, -2)
    names_row = jnp.zeros((count, BLK_DEV, GHOST), bool)
    names_column = jnp.zeros((count, BLK_DEV, GHOST), bool)
    for b in range(NB):
        names_row |= live[:, :, b, None] == ghost_ids[:, None, :]
        names_column |= live[:, :, b, None] == ghost_slots[:, None, :]
    need = jnp.any(names_row & names_column, axis=1)
    segment = np.repeat(np.arange(len(groups)), full)
    before = (segment[:, None] == segment[None, :]) & (np.arange(GHOST)[:, None] < np.arange(GHOST)[None, :])
    ones = need.astype(jnp.bfloat16)
    rank = jnp.dot(ones, jnp.asarray(before, jnp.bfloat16), preferred_element_type=jnp.float32).astype(jnp.int32)
    over = jnp.zeros((count, GHOST), jnp.int32)
    for caps in tiers(along_gy)[:-1]:
        limit = jnp.asarray(np.repeat(caps, full).astype(np.int32))
        over += (need & (rank >= limit)).astype(jnp.int32)
    tier = jnp.max(over)
    ranked = jnp.where(need, rank, -1)

    own_rank = lax.dynamic_index_in_dim(ranked, gx_index * along_gy + gy_index, 0, keepdims=False)
    by_device = ranked.reshape(along_gx, along_gy, GHOST)
    sent_rank = jnp.concatenate(
        [jnp.roll(by_device[:, :, lo:hi], (s, t), (0, 1)) for (s, t), lo, hi in zip([DIRS[g[0]] for g in groups], bounds[:-1], bounds[1:])],
        axis=2,
    ).reshape(count, GHOST)
    sent_rank = lax.dynamic_index_in_dim(sent_rank, gx_index * along_gy + gy_index, 0, keepdims=False)
    block = np.concatenate([[1 + r * NB + c for r in rows for c in range(NB)] for rows in ROWS])
    chosen = (sent_rank[:, None] == jnp.arange(widest, dtype=jnp.int32)[None, :]).astype(jnp.bfloat16)
    weights = (segment[None, :] == np.arange(len(groups))[:, None]) * block[None, :]
    sends = jnp.dot(jnp.asarray(weights, jnp.bfloat16), chosen, preferred_element_type=jnp.float32)
    sends = sends.astype(jnp.int32)

    me = gx_index * along_gy + gy_index
    own_slots = lax.dynamic_index_in_dim(slots, me, 0, keepdims=False)
    my_ghost_slots = lax.dynamic_index_in_dim(ghost_slots, me, 0, keepdims=False)
    my_ghost_ids = lax.dynamic_index_in_dim(ghost_ids, me, 0, keepdims=False)
    flat_slots = jnp.concatenate([own_slots.reshape(-1), my_ghost_slots])
    row_ids = jnp.concatenate([jnp.repeat(me * BLK_DEV + jnp.arange(BLK_DEV, dtype=jnp.int32), NB), my_ghost_ids])
    wanted = jnp.where(own_slots >= 0, own_slots, -2)
    of_row = wanted[:, :, None] == row_ids[None, None, :]
    of_column = wanted[:, :, None] == flat_slots[None, None, :]

    def places(caps):
        offset = np.repeat(starts_of(caps)[:-1], full) + 1 + OWN
        ghost = jnp.where(own_rank >= 0, own_rank + jnp.asarray(offset, jnp.int32), 0)
        place = jnp.concatenate([1 + jnp.arange(OWN, dtype=jnp.int32), ghost])
        both = of_row[:, :, None, :] & of_column[:, None, :, :]
        return jnp.sum(jnp.where(both, place[None, None, None, :], 0), axis=3).reshape(-1)

    def send_list(caps):
        return jnp.concatenate([sends[d, :cap] for d, cap in enumerate(caps)])

    return tier, places, send_list


def purify(sizes, caps, place_ref, send_ref, kernel_ref, margin_ref, ham_ref, out_ref,
           blocks, other, lead, cubic, out_box, in_box, send_sem, recv_sem):
    along_gx, along_gy = sizes
    pair_starts = [v // 2 for v in starts_of(caps)]
    pairs = pair_starts[-1]
    gx_index, gy_index = lax.axis_index("gx"), lax.axis_index("gy")
    served = [DIRS[group[0]] for group in messages(along_gy)]
    targets = [
        (lax.rem(gx_index - s + along_gx, along_gx), lax.rem(gy_index - t + along_gy, along_gy)) for s, t in served
    ]
    low = lax.broadcasted_iota(jnp.int32, (BS, 2 * BS), 1) < BS

    def keep_row(into, at, values):
        for c in range(values.shape[1] // BS):
            block = values[:, c * BS : (c + 1) * BS]
            into[at + c] = jnp.concatenate([block, block], axis=1)

    def own(source, into):
        @pl.loop(0, BLK_DEV)
        def _(i):
            rows = pl.ds(pl.multiple_of(i * BS, BS), BS)
            keep_row(into, 1 + i * NB, source[rows, :])

    def exchange(turn, source):
        slot = turn % 2

        @pl.loop(0, pairs // 4)
        def _(h):
            loaded = [source[send_ref[8 * h + j]] for j in range(8)]
            for j in range(4):
                out_box[slot, 4 * h + j] = jnp.where(low, loaded[2 * j], loaded[2 * j + 1])

        copies = []
        for d, target in enumerate(targets):
            part = pl.ds(pair_starts[d], pair_starts[d + 1] - pair_starts[d])
            copies.append(
                pltpu.make_async_remote_copy(
                    src_ref=out_box.at[slot, part],
                    dst_ref=in_box.at[turn, part],
                    send_sem=send_sem.at[turn, d],
                    recv_sem=recv_sem.at[turn, d],
                    device_id=target,
                    device_id_type=pl.DeviceIdType.MESH,
                )
            )
        return copies

    def arrive(turn, copies, into):
        for copy in copies:
            copy.wait_recv()

        @pl.loop(0, pairs // 4)
        def _(h):
            loaded = [in_box[turn, 4 * h + j] for j in range(4)]
            for j in range(4):
                keep_row(into, 1 + OWN + 8 * h + 2 * j, loaded[j])

    def product(left, right, finish):
        @pl.loop(0, BLK_DEV)
        def _(i):
            rows = pl.ds(pl.multiple_of(i * BS, BS), BS)
            left_rows = left[rows, :]
            for half in range(2):
                wide = []
                for b in (4 * half, 4 * half + 2):
                    tall = []
                    for a in range(NB):
                        at = (i * NB + a) * NB + b
                        tall.append(jnp.where(low, right[place_ref[at]], right[place_ref[at + 1]]))
                    wide.append(jnp.concatenate(tall, axis=0))
                result = jnp.dot(left_rows, jnp.concatenate(wide, axis=1), preferred_element_type=jnp.float32)
                finish(i, half, rows, slice(4 * half * BS, 4 * (half + 1) * BS), result)

    def put_lead(i, half, rows, cols, result):
        lead[rows, cols] = result.astype(jnp.bfloat16)

    def put_cubic(i, half, rows, cols, result):
        value = result.astype(jnp.bfloat16)
        cubic[rows, cols] = value
        keep_row(blocks, 1 + i * NB + 4 * half, value)

    def put_purified(i, half, rows, cols, result):
        value = 3.0 * cubic[rows, cols].astype(jnp.float32) - 2.0 * result
        keep_row(other, 1 + i * NB + 4 * half, value.astype(jnp.bfloat16))

    def put_out(i, half, rows, cols, result):
        out_ref[rows, cols] = result

    def begin(copies):
        for _, copy in sorted(enumerate(copies), key=lambda entry: (served[entry[0]][1] == 0, entry[0])):
            copy.start()

    barrier = pltpu.get_barrier_semaphore()
    for target in targets:
        pl.semaphore_signal(barrier, inc=1, device_id=target, device_id_type=pl.DeviceIdType.MESH)
    zero = jnp.zeros((BS, 2 * BS), jnp.bfloat16)
    blocks[0] = zero
    other[0] = zero
    own(margin_ref, blocks)
    first = exchange(0, blocks)
    pl.semaphore_wait(barrier, len(targets))
    begin(first)
    own(kernel_ref, other)
    second = exchange(1, other)
    begin(second)
    arrive(0, first, blocks)
    product(kernel_ref, blocks, put_lead)
    arrive(1, second, other)
    product(lead, other, put_cubic)
    for copy in first:
        copy.wait_send()
    third = exchange(2, blocks)
    begin(third)
    arrive(2, third, blocks)
    product(lead, blocks, put_purified)
    for copy in second:
        copy.wait_send()
    fourth = exchange(3, other)
    begin(fourth)
    arrive(3, fourth, other)
    product(ham_ref, other, put_out)
    for copy in third + fourth:
        copy.wait_send()


def call(sizes, caps, collective_id, places, send_list, kernel, margin, hamiltonian):
    pairs = sum(caps) // 2
    rows, width = kernel.shape
    in_vmem = pl.BlockSpec(memory_space=pltpu.VMEM)
    in_smem = pl.BlockSpec(memory_space=pltpu.SMEM)
    block_count = 1 + OWN + sum(caps)
    return pl.pallas_call(
        functools.partial(purify, sizes, caps),
        out_shape=jax.ShapeDtypeStruct((rows, width), jnp.float32),
        in_specs=[in_smem, in_smem, in_vmem, in_vmem, in_vmem],
        out_specs=in_vmem,
        scratch_shapes=[
            pltpu.VMEM((block_count, BS, 2 * BS), jnp.bfloat16),
            pltpu.VMEM((block_count, BS, 2 * BS), jnp.bfloat16),
            pltpu.VMEM((rows, width), jnp.bfloat16),
            pltpu.VMEM((rows, width), jnp.bfloat16),
            pltpu.VMEM((2, pairs, BS, 2 * BS), jnp.bfloat16),
            pltpu.VMEM((4, pairs, BS, 2 * BS), jnp.bfloat16),
            pltpu.SemaphoreType.DMA((4, len(caps))),
            pltpu.SemaphoreType.DMA((4, len(caps))),
        ],
        compiler_params=pltpu.CompilerParams(
            collective_id=collective_id, has_side_effects=True, vmem_limit_bytes=56 * 2**20
        ),
    )(places, send_list, kernel, margin, hamiltonian)


def body(sizes, kernel, margin, hamiltonian, columns):
    tier, places, send_list = tables(columns, *sizes, lax.axis_index("gx"), lax.axis_index("gy"))

    def run(caps, collective_id):
        return lambda: call(
            sizes, caps, collective_id, places(caps), send_list(caps), kernel, margin, hamiltonian
        )

    return lax.switch(tier, [run(caps, n) for n, caps in enumerate(tiers(sizes[1]))])


def solution(mesh):
    sizes = (mesh.shape["gx"], mesh.shape["gy"])
    in_specs = (P(("gx", "gy"), None), P(("gx", "gy"), None), P(("gx", "gy"), None), P())
    out_specs = P(("gx", "gy"), None)
    return jax.shard_map(
        functools.partial(body, sizes), mesh=mesh, in_specs=in_specs, out_specs=out_specs, check_vma=False
    )
```

```python
import functools

import jax
import jax.numpy as jnp
import numpy as np
from jax import lax
from jax.experimental import pallas as pl
from jax.experimental.pallas import tpu as pltpu
from jax.sharding import PartitionSpec as P

BS = 64
NB = 8
EDGE = 4
BLK_DEV = 16
OWN = BLK_DEV * NB
DIRS = ((0, -1), (0, 1), (-1, 0), (1, 0), (-1, -1), (-1, 1), (1, -1), (1, 1))
CORNERS = {-1: (1,), 0: (0, 1), 1: (0,)}


def direction_rows(s, t):
    return [EDGE * (2 * p + q) + r for p in CORNERS[s] for q in CORNERS[t] for r in range(EDGE)]


ROWS = [direction_rows(s, t) for s, t in DIRS]
SIZES = [len(rows) * NB for rows in ROWS]
GHOST = sum(SIZES)


def messages(along_gy):
    if along_gy == 2:
        return ((0, 1), (2,), (3,), (4, 5), (6, 7))
    return tuple((d,) for d in range(len(DIRS)))


def full_caps(along_gy):
    return tuple(sum(SIZES[d] for d in group) for group in messages(along_gy))


def tiers(along_gy):
    if along_gy == 2:
        return (40, 24, 24, 16, 16), (44, 24, 24, 18, 18), (56, 28, 28, 24, 24), full_caps(along_gy)
    return (28, 28, 20, 20, 14, 14, 14, 14), (40, 40, 32, 32, 20, 20, 20, 20), full_caps(along_gy)


def starts_of(caps):
    return [int(v) for v in np.cumsum((0,) + caps)]


def tables(columns, along_gx, along_gy, gx_index, gy_index):
    count = along_gx * along_gy
    groups, full = messages(along_gy), full_caps(along_gy)
    bounds = starts_of(full)
    widest = max(full)
    ids = np.arange(count * BLK_DEV, dtype=np.int32).reshape(along_gx, along_gy, BLK_DEV)
    ids = np.repeat(ids, NB, axis=2)
    lanes = columns.reshape(along_gx, along_gy, OWN)

    def ghosts(lib, source):
        kept = []
        for (s, t), rows in zip(DIRS, ROWS):
            moved = lib.roll(source, (-s, -t), (0, 1))
            kept += [moved[:, :, r * NB : (r + EDGE) * NB] for r in rows[::EDGE]]
        return lib.concatenate(kept, axis=2).reshape(count, GHOST)

    ghost_ids = jnp.asarray(ghosts(np, ids))
    ghost_slots = ghosts(jnp, lanes)
    slots = columns.reshape(count, BLK_DEV, NB)
    live = jnp.where(slots >= 0, slots, -2)
    names_row = jnp.zeros((count, BLK_DEV, GHOST), bool)
    names_column = jnp.zeros((count, BLK_DEV, GHOST), bool)
    for b in range(NB):
        names_row |= live[:, :, b, None] == ghost_ids[:, None, :]
        names_column |= live[:, :, b, None] == ghost_slots[:, None, :]
    need = jnp.any(names_row & names_column, axis=1)
    segment = np.repeat(np.arange(len(groups)), full)
    before = (segment[:, None] == segment[None, :]) & (np.arange(GHOST)[:, None] < np.arange(GHOST)[None, :])
    ones = need.astype(jnp.bfloat16)
    rank = jnp.dot(ones, jnp.asarray(before, jnp.bfloat16), preferred_element_type=jnp.float32).astype(jnp.int32)
    over = jnp.zeros((count, GHOST), jnp.int32)
    for caps in tiers(along_gy)[:-1]:
        limit = jnp.asarray(np.repeat(caps, full).astype(np.int32))
        over += (need & (rank >= limit)).astype(jnp.int32)
    tier = jnp.max(over)
    ranked = jnp.where(need, rank, -1)

    own_rank = lax.dynamic_index_in_dim(ranked, gx_index * along_gy + gy_index, 0, keepdims=False)
    by_device = ranked.reshape(along_gx, along_gy, GHOST)
    sent_rank = jnp.concatenate(
        [jnp.roll(by_device[:, :, lo:hi], (s, t), (0, 1)) for (s, t), lo, hi in zip([DIRS[g[0]] for g in groups], bounds[:-1], bounds[1:])],
        axis=2,
    ).reshape(count, GHOST)
    sent_rank = lax.dynamic_index_in_dim(sent_rank, gx_index * along_gy + gy_index, 0, keepdims=False)
    block = np.concatenate([[1 + r * NB + c for r in rows for c in range(NB)] for rows in ROWS])
    chosen = (sent_rank[:, None] == jnp.arange(widest, dtype=jnp.int32)[None, :]).astype(jnp.bfloat16)
    weights = (segment[None, :] == np.arange(len(groups))[:, None]) * block[None, :]
    sends = jnp.dot(jnp.asarray(weights, jnp.bfloat16), chosen, preferred_element_type=jnp.float32)
    sends = sends.astype(jnp.int32)

    me = gx_index * along_gy + gy_index
    own_slots = lax.dynamic_index_in_dim(slots, me, 0, keepdims=False)
    my_ghost_slots = lax.dynamic_index_in_dim(ghost_slots, me, 0, keepdims=False)
    my_ghost_ids = lax.dynamic_index_in_dim(ghost_ids, me, 0, keepdims=False)
    flat_slots = jnp.concatenate([own_slots.reshape(-1), my_ghost_slots])
    row_ids = jnp.concatenate([jnp.repeat(me * BLK_DEV + jnp.arange(BLK_DEV, dtype=jnp.int32), NB), my_ghost_ids])
    wanted = jnp.where(own_slots >= 0, own_slots, -2)
    of_row = wanted[:, :, None] == row_ids[None, None, :]
    of_column = wanted[:, :, None] == flat_slots[None, None, :]

    def places(caps):
        offset = np.repeat(starts_of(caps)[:-1], full) + 1 + OWN
        ghost = jnp.where(own_rank >= 0, own_rank + jnp.asarray(offset, jnp.int32), 0)
        place = jnp.concatenate([1 + jnp.arange(OWN, dtype=jnp.int32), ghost])
        both = of_row[:, :, None, :] & of_column[:, None, :, :]
        return jnp.sum(jnp.where(both, place[None, None, None, :], 0), axis=3).reshape(-1)

    def send_list(caps):
        return jnp.concatenate([sends[d, :cap] for d, cap in enumerate(caps)])

    return tier, places, send_list


def purify(sizes, caps, place_ref, send_ref, kernel_ref, margin_ref, ham_ref, out_ref,
           blocks, other, lead, cubic, out_box, in_box, send_sem, recv_sem):
    along_gx, along_gy = sizes
    pair_starts = [v // 2 for v in starts_of(caps)]
    pairs = pair_starts[-1]
    gx_index, gy_index = lax.axis_index("gx"), lax.axis_index("gy")
    served = [DIRS[group[0]] for group in messages(along_gy)]
    targets = [
        (lax.rem(gx_index - s + along_gx, along_gx), lax.rem(gy_index - t + along_gy, along_gy)) for s, t in served
    ]
    low = lax.broadcasted_iota(jnp.int32, (BS, 2 * BS), 1) < BS

    def keep_row(into, at, values):
        for c in range(values.shape[1] // BS):
            block = values[:, c * BS : (c + 1) * BS]
            into[at + c] = jnp.concatenate([block, block], axis=1)

    def own(source, into):
        @pl.loop(0, BLK_DEV)
        def _(i):
            rows = pl.ds(pl.multiple_of(i * BS, BS), BS)
            keep_row(into, 1 + i * NB, source[rows, :])

    def exchange(turn, source):
        slot = turn % 2

        @pl.loop(0, pairs // 4)
        def _(h):
            loaded = [source[send_ref[8 * h + j]] for j in range(8)]
            for j in range(4):
                out_box[slot, 4 * h + j] = jnp.where(low, loaded[2 * j], loaded[2 * j + 1])

        copies = []
        for d, target in enumerate(targets):
            part = pl.ds(pair_starts[d], pair_starts[d + 1] - pair_starts[d])
            copies.append(
                pltpu.make_async_remote_copy(
                    src_ref=out_box.at[slot, part],
                    dst_ref=in_box.at[turn, part],
                    send_sem=send_sem.at[turn, d],
                    recv_sem=recv_sem.at[turn, d],
                    device_id=target,
                    device_id_type=pl.DeviceIdType.MESH,
                )
            )
        return copies

    def arrive(turn, copies, into):
        for copy in copies:
            copy.wait_recv()

        @pl.loop(0, pairs // 4)
        def _(h):
            loaded = [in_box[turn, 4 * h + j] for j in range(4)]
            for j in range(4):
                keep_row(into, 1 + OWN + 8 * h + 2 * j, loaded[j])

    def product(left, right, finish):
        @pl.loop(0, BLK_DEV)
        def _(i):
            rows = pl.ds(pl.multiple_of(i * BS, BS), BS)
            left_rows = left[rows, :]
            for half in range(2):
                wide = []
                for b in (4 * half, 4 * half + 2):
                    tall = []
                    for a in range(NB):
                        at = (i * NB + a) * NB + b
                        tall.append(jnp.where(low, right[place_ref[at]], right[place_ref[at + 1]]))
                    wide.append(jnp.concatenate(tall, axis=0))
                result = jnp.dot(left_rows, jnp.concatenate(wide, axis=1), preferred_element_type=jnp.float32)
                finish(i, half, rows, slice(4 * half * BS, 4 * (half + 1) * BS), result)

    def put_lead(i, half, rows, cols, result):
        lead[rows, cols] = result.astype(jnp.bfloat16)

    def put_cubic(i, half, rows, cols, result):
        value = result.astype(jnp.bfloat16)
        cubic[rows, cols] = value
        keep_row(blocks, 1 + i * NB + 4 * half, value)

    def put_purified(i, half, rows, cols, result):
        value = 3.0 * cubic[rows, cols].astype(jnp.float32) - 2.0 * result
        keep_row(other, 1 + i * NB + 4 * half, value.astype(jnp.bfloat16))

    def put_out(i, half, rows, cols, result):
        out_ref[rows, cols] = result

    def begin(copies):
        for _, copy in sorted(enumerate(copies), key=lambda entry: (served[entry[0]][1] == 0, entry[0])):
            copy.start()

    barrier = pltpu.get_barrier_semaphore()
    for target in targets:
        pl.semaphore_signal(barrier, inc=1, device_id=target, device_id_type=pl.DeviceIdType.MESH)
    zero = jnp.zeros((BS, 2 * BS), jnp.bfloat16)
    blocks[0] = zero
    other[0] = zero
    own(margin_ref, blocks)
    first = exchange(0, blocks)
    pl.semaphore_wait(barrier, len(targets))
    begin(first)
    own(kernel_ref, other)
    second = exchange(1, other)
    begin(second)
    arrive(0, first, blocks)
    product(kernel_ref, blocks, put_lead)
    arrive(1, second, other)
    product(lead, other, put_cubic)
    for copy in first:
        copy.wait_send()
    third = exchange(2, blocks)
    begin(third)
    arrive(2, third, blocks)
    product(lead, blocks, put_purified)
    for copy in second:
        copy.wait_send()
    fourth = exchange(3, other)
    begin(fourth)
    arrive(3, fourth, other)
    product(ham_ref, other, put_out)
    for copy in third + fourth:
        copy.wait_send()


def call(sizes, caps, collective_id, places, send_list, kernel, margin, hamiltonian):
    pairs = sum(caps) // 2
    rows, width = kernel.shape
    in_vmem = pl.BlockSpec(memory_space=pltpu.VMEM)
    in_smem = pl.BlockSpec(memory_space=pltpu.SMEM)
    block_count = 1 + OWN + sum(caps)
    return pl.pallas_call(
        functools.partial(purify, sizes, caps),
        out_shape=jax.ShapeDtypeStruct((rows, width), jnp.float32),
        in_specs=[in_smem, in_smem, in_vmem, in_vmem, in_vmem],
        out_specs=in_vmem,
        scratch_shapes=[
            pltpu.VMEM((block_count, BS, 2 * BS), jnp.bfloat16),
            pltpu.VMEM((block_count, BS, 2 * BS), jnp.bfloat16),
            pltpu.VMEM((rows, width), jnp.bfloat16),
            pltpu.VMEM((rows, width), jnp.bfloat16),
            pltpu.VMEM((2, pairs, BS, 2 * BS), jnp.bfloat16),
            pltpu.VMEM((4, pairs, BS, 2 * BS), jnp.bfloat16),
            pltpu.SemaphoreType.DMA((4, len(caps))),
            pltpu.SemaphoreType.DMA((4, len(caps))),
        ],
        compiler_params=pltpu.CompilerParams(
            collective_id=collective_id, has_side_effects=True, vmem_limit_bytes=56 * 2**20
        ),
    )(places, send_list, kernel, margin, hamiltonian)


def body(sizes, kernel, margin, hamiltonian, columns):
    tier, places, send_list = tables(columns, *sizes, lax.axis_index("gx"), lax.axis_index("gy"))

    def run(caps, collective_id):
        return lambda: call(
            sizes, caps, collective_id, places(caps), send_list(caps), kernel, margin, hamiltonian
        )

    return lax.switch(tier, [run(caps, n) for n, caps in enumerate(tiers(sizes[1]))])


def solution(mesh):
    sizes = (mesh.shape["gx"], mesh.shape["gy"])
    in_specs = (P(("gx", "gy"), None), P(("gx", "gy"), None), P(("gx", "gy"), None), P())
    out_specs = P(("gx", "gy"), None)
    return jax.shard_map(
        functools.partial(body, sizes), mesh=mesh, in_specs=in_specs, out_specs=out_specs, check_vma=False
    )
```
